32 devices in a mesh: seq: 16 (over z, y, core), fsdp: 2 (over x).
Axes of the slice: x: 2, y: 2, z: 4, core: 2. Of those that a mesh axis runs over, the one named last changes fastest.
Arguments:
- inputs: bfloat16 [2, 4096, 1024], P('fsdp', 'seq'), may hold values from -6.5 to 6.5
- segments: int32 [2, 4096], P('fsdp', 'seq'), may hold values from 0 to 2, as said below
- norm_gain: bfloat16 [1024], P('fsdp'), may hold values from 0.5 to 1.5
- qkv_weight: bfloat16 [1024, 2048], P('fsdp'), may hold values from -0.1875 to 0.1875
- gate_weight: bfloat16 [1024, 1024], P('fsdp'), may hold values from -0.1875 to 0.1875
- mix_weight: bfloat16 [1024, 8], P('fsdp'), may hold values from -1 to 1
- conv_weight: bfloat16 [2048, 4], P('fsdp'), may hold values from -3 to 3
- decay_log: float32 [4], replicated, may hold values from 0 to 2.77
- decay_bias: float32 [4], replicated, may hold values from -10.5 to -2
- head_gain: bfloat16 [256], P('fsdp'), may hold values from 0.5 to 1.5
- out_weight: bfloat16 [1024, 1024], P('fsdp'), may hold values from -0.25 to 0.25
- ffn_gain: bfloat16 [1024], P('fsdp'), may hold values from 0.5 to 1.5
- hidden_gate: bfloat16 [1024, 2816], P('fsdp'), may hold values from -0.1875 to 0.1875
- hidden_up: bfloat16 [1024, 2816], P('fsdp'), may hold values from -0.1875 to 0.1875
- hidden_down: bfloat16 [2816, 1024], P('fsdp'), may hold values from -0.15625 to 0.15625
- cotangent: bfloat16 [2, 4096, 1024], P('fsdp', 'seq'), may hold values from -6 to 6
Outputs:
- outputs: bfloat16 [2, 4096, 1024], P('fsdp', 'seq')
- input_grad: float32 [2, 4096, 1024], P('fsdp', 'seq')
- grad_norm_gain: float32 [1024], P('fsdp')
- grad_qkv_weight: float32 [1024, 2048], P('fsdp', 'seq')
- grad_gate_weight: float32 [1024, 1024], P('fsdp', 'seq')
- grad_mix_weight: float32 [1024, 8], P('fsdp')
- grad_conv_weight: float32 [2048, 4], P('fsdp')
- grad_decay_log: float32 [4], replicated
- grad_decay_bias: float32 [4], replicated
- grad_head_gain: float32 [256], P('fsdp')
- grad_out_weight: float32 [1024, 1024], P('fsdp', 'seq')
- grad_ffn_gain: float32 [1024], P('fsdp')
- grad_hidden_gate: float32 [1024, 2816], P('fsdp', 'seq')
- grad_hidden_up: float32 [1024, 2816], P('fsdp', 'seq')
- grad_hidden_down: float32 [2816, 1024], P('fsdp', 'seq')
The draws below stay inside these ranges and needn't reach their ends.
Inputs may be any that keep to these rules, and one draw needn't show every extreme that they name: `segments`: within each pack the ids never fall and rise by one at each change, starting at 0.
All inputs are finite; a program needn't handle non-finite values.
Results may differ from the reference program's by a relative error of at most 0.013.
Values may be sent and summed in bfloat16 or wider, within the bound.
A program may use at most 256 MiB of HBM per device.

```python
import jax
import jax.numpy as jnp
from jax import lax

D = 1024
H = 4
DK = 128
DV = 256
FF = 2816
CONV = 4
GROUP = 64
TOK_DEV = 256
SEQLEN = 4096
PACKS = 2
VD = 1024
QKV = 2048


offset_share = 0.5


def offset_signs(key):
    picked = jax.random.bernoulli(jax.random.fold_in(key, 101), 0.5, (D,))
    return picked.astype(jnp.float32) * 2.0 - 1.0


def slow_heads(key):
    chosen = jax.random.randint(jax.random.fold_in(key, 202), (), 0, H)
    return lax.broadcasted_iota(jnp.int32, (H,), 0) == chosen


def draw_segments(key, part):
    key = jax.random.fold_in(key, 11)
    first_key, last_key = jax.random.split(key)
    starts = jax.random.randint(first_key, (PACKS, 1), 1, TOK_DEV // 2 + 1)
    finish = jax.random.randint(last_key, (PACKS, 1), SEQLEN - TOK_DEV // 2, SEQLEN)
    places = lax.broadcasted_iota(jnp.int32, (PACKS, SEQLEN), 1)
    return (places >= starts).astype(jnp.int32) + (places >= finish).astype(jnp.int32)


def draw_inputs(key, part):
    signs = offset_signs(key)
    key = jax.random.fold_in(key, 3)
    noise = jax.random.truncated_normal(key, -6.0, 6.0, (PACKS, SEQLEN, D), jnp.float32)
    return (offset_share * signs + noise).astype(jnp.bfloat16)


def draw_mix_weight(key, part):
    signs = offset_signs(key)
    key = jax.random.fold_in(key, 5)
    main_key, target_key = jax.random.split(key)
    random_part = jax.random.truncated_normal(main_key, -4.0, 4.0, (D, 2 * H), jnp.float32) * D ** (-0.5)
    targets = jax.random.uniform(target_key, (H,), jnp.float32, 2.5, 3.5)
    factor = (1.0 + offset_share * offset_share) ** 0.5 / (offset_share * D)
    shift = jnp.concatenate([jnp.zeros((H,), jnp.float32), -targets * factor])
    return (random_part + signs[:, None] * shift[None, :]).astype(jnp.bfloat16)


def draw_decay_log(key, part):
    slow = slow_heads(key)
    key = jax.random.fold_in(key, 7)
    unit = jax.random.uniform(key, (H,), jnp.float32)
    return jnp.where(slow, 0.5 * unit, 2.77 * unit)


def draw_decay_bias(key, part):
    slow = slow_heads(key)
    key = jax.random.fold_in(key, 9)
    unit = jax.random.uniform(key, (H,), jnp.float32)
    others = -6.0 + 4.0 * unit
    return jnp.where(slow, -10.5 + unit, others)


def block_scale(key, shape, shards, low, high):
    loudness, own = 1.0, jax.random.fold_in(key, 6)
    for position, parts in shards:
        steps = jnp.exp(jax.random.uniform(jax.random.fold_in(own, position), (parts,), jnp.float32, low / len(shards), high / len(shards)))
        loudness = loudness * jnp.repeat(steps, shape[position] // parts).reshape([-1 if axis == position else 1 for axis in range(len(shape))])
    return loudness


def normal_values(rng, dims, scale, reach, cuts=(), held_as=jnp.bfloat16):
    loudness = block_scale(rng, dims, cuts, -0.22, 0.18) if cuts else 1.0
    entries = jax.random.normal(rng, dims, jnp.float32) * scale * loudness
    return jnp.minimum(jnp.maximum(entries, -reach), reach).astype(held_as)


def setup_inputs(seed: int = 0) -> dict:
    seeds = jax.random.split(jax.random.key(seed), 17)
    return {
        "inputs": draw_inputs(jax.random.fold_in(seeds[16], 71), 0),
        "segments": draw_segments(jax.random.fold_in(seeds[16], 71), 0),
        "norm_gain": jnp.clip(1.0 + 0.1 * jax.random.normal(seeds[2], (D,), jnp.float32), 0.5, 1.5).astype(jnp.bfloat16),
        "qkv_weight": normal_values(seeds[3], (D, QKV), D ** -0.5, 0.1875, ((0, 2),)),
        "gate_weight": normal_values(seeds[4], (D, VD), D ** -0.5, 0.1875, ((0, 2),)),
        "mix_weight": draw_mix_weight(jax.random.fold_in(seeds[16], 71), 0),
        "conv_weight": normal_values(seeds[6], (QKV, CONV), CONV ** -0.5, 3.0, ((0, 2),)),
        "decay_log": draw_decay_log(jax.random.fold_in(seeds[16], 71), 0),
        "decay_bias": draw_decay_bias(jax.random.fold_in(seeds[16], 71), 0),
        "head_gain": jnp.clip(1.0 + 0.1 * jax.random.normal(seeds[9], (DV,), jnp.float32), 0.5, 1.5).astype(jnp.bfloat16),
        "out_weight": normal_values(seeds[10], (VD, D), (VD // 2) ** -0.5, 0.25, ((0, 2),)),
        "ffn_gain": jnp.clip(1.0 + 0.1 * jax.random.normal(seeds[11], (D,), jnp.float32), 0.5, 1.5).astype(jnp.bfloat16),
        "hidden_gate": normal_values(seeds[12], (D, FF), D ** -0.5, 0.1875, ((0, 2),)),
        "hidden_up": normal_values(seeds[13], (D, FF), D ** -0.5, 0.1875, ((0, 2),)),
        "hidden_down": normal_values(seeds[14], (FF, D), (FF // 2) ** -0.5, 0.15625, ((0, 2),)),
        "cotangent": normal_values(seeds[15], (PACKS, SEQLEN, D), 1.0, 6.0, ((0, 2), (1, 16))),
    }


norm_eps = 1e-06
highest = lax.Precision.HIGHEST

@jax.custom_vjp
def low(v):
    return lax.optimization_barrier(v.astype(jnp.bfloat16)).astype(jnp.float32)

@jax.custom_vjp
def low_back(v):
    return v

def low_keep(v):
    return (low(v), None)

def low_pass(kept, grad):
    return (grad,)

def back_keep(v):
    return (v, None)

def back_low(kept, grad):
    return (low(grad),)
low.defvjp(low_keep, low_pass)
low_back.defvjp(back_keep, back_low)

def rms_norm(values, gain_vec):
    return values * lax.rsqrt(lax.optimization_barrier(jnp.mean(values * values, axis=-1, keepdims=True)) + norm_eps) * gain_vec

def prepare(key_rows, value_rows, beta_rows, decay_rows, seg_now, seg_prev):
    block_len = key_rows.shape[1]
    row_index = lax.broadcasted_iota(jnp.int32, (block_len, block_len), 0)
    col_index = lax.broadcasted_iota(jnp.int32, (block_len, block_len), 1)
    totals = jnp.swapaxes(jnp.cumsum(decay_rows, axis=1), 1, 2)
    same_doc = ((seg_now[:, :, None] == seg_now[:, None, :]) & (col_index <= row_index)[None])[:, None]
    spread = totals[:, :, :, None] - totals[:, :, None, :]
    weight = jnp.where(same_doc, jnp.exp(jnp.where(same_doc, spread, 0.0)), 0.0)
    keep_prev = (seg_now == seg_prev[:, None]).astype(totals.dtype)
    start_gain = jnp.exp(totals) * keep_prev[:, None, :]
    key_heads = jnp.swapaxes(key_rows, 1, 2)
    value_heads = jnp.swapaxes(value_rows, 1, 2)
    beta_heads = jnp.swapaxes(beta_rows, 1, 2)
    key_inner = jnp.einsum('phik,phjk->phij', key_heads, key_heads, precision=highest)
    strict_part = jnp.where((col_index < row_index)[None, None], weight * key_inner * beta_heads[:, :, None, :], 0.0)
    system = strict_part + jnp.eye(block_len, dtype=strict_part.dtype)
    right_side = jnp.concatenate([value_heads, start_gain[..., None] * key_heads], axis=-1)
    solved = jax.scipy.linalg.solve_triangular(system, right_side, lower=True, unit_diagonal=True)
    value_width = value_heads.shape[-1]
    tail_weight = weight[:, :, -1, :] * beta_heads
    return (key_heads, beta_heads, weight, start_gain, solved[..., :value_width], solved[..., value_width:], tail_weight)

def block_core(queries, key_rows, value_rows, beta_rows, decay_rows, seg_now, seg_prev, state_in):
    key_heads, beta_heads, weight, start_gain, base_part, wide_part, tail_weight = prepare(key_rows, value_rows, beta_rows, decay_rows, seg_now, seg_prev)
    query_heads = jnp.swapaxes(queries, 1, 2)
    fixed_part = base_part - jnp.einsum('phck,phkv->phcv', wide_part, state_in, precision=highest)
    scores = weight * jnp.einsum('phik,phjk->phij', query_heads, key_heads, precision=highest)
    block_out = start_gain[..., None] * jnp.einsum('phck,phkv->phcv', query_heads, state_in, precision=highest)
    block_out = block_out + jnp.einsum('phij,phjv->phiv', scores, beta_heads[..., None] * fixed_part, precision=highest)
    new_state = start_gain[:, :, -1, None, None] * state_in + jnp.einsum('phck,phcv->phkv', key_heads * tail_weight[..., None], fixed_part, precision=highest)
    return (jnp.swapaxes(block_out, 1, 2), new_state)

def block_inputs(queries, key_rows, value_rows, beta_rows, decay_rows, segments, first_prev):
    pack_count, length_all = segments.shape
    block_count = length_all // GROUP

    def to_blocks(array):
        return jnp.swapaxes(array.reshape((pack_count, block_count, GROUP) + array.shape[2:]), 0, 1)
    last_segs = segments[:, GROUP - 1::GROUP]
    prev_segs = jnp.concatenate([first_prev[:, None], last_segs[:, :-1]], axis=1)
    return (to_blocks(queries), to_blocks(key_rows), to_blocks(value_rows), to_blocks(beta_rows), to_blocks(decay_rows), to_blocks(segments), jnp.swapaxes(prev_segs, 0, 1))

def run_blocks(queries, key_rows, value_rows, beta_rows, decay_rows, segments, state_in, first_prev):
    stacked = block_inputs(queries, key_rows, value_rows, beta_rows, decay_rows, segments, first_prev)

    def advance(carry, block_in):
        block_out, new_state = block_core(*block_in, carry)
        return (new_state, block_out)
    final_state, block_outs = lax.scan(jax.checkpoint(advance), state_in, stacked)
    readout = jnp.swapaxes(block_outs, 0, 1)
    return (readout.reshape(queries.shape[:2] + readout.shape[-2:]), final_state)

def front_end(extended, conv_weight, coeffs, decay_log, decay_bias, ext_segs, segments):
    length_all = segments.shape[1]
    summed = jnp.zeros(extended.shape[:1] + (length_all,) + extended.shape[2:], extended.dtype)
    for offset in range(CONV):
        window = extended[:, offset:offset + length_all]
        same_seg = (ext_segs[:, offset:offset + length_all] == segments)[..., None]
        summed = summed + conv_weight[:, offset] * jnp.where(same_seg, window, 0.0)
    activated = jax.nn.silu(summed)
    lead_shape = activated.shape[:2]
    key_span = H * DK
    queries = activated[..., :key_span].reshape(lead_shape + (H, DK))
    key_rows = activated[..., key_span:2 * key_span].reshape(lead_shape + (H, DK))
    value_rows = activated[..., 2 * key_span:].reshape(lead_shape + (H, DV))
    queries = queries * lax.rsqrt(lax.optimization_barrier(jnp.sum(queries * queries, axis=-1, keepdims=True)) + norm_eps) * DK ** (-0.5)
    key_rows = key_rows * lax.rsqrt(lax.optimization_barrier(jnp.sum(key_rows * key_rows, axis=-1, keepdims=True)) + norm_eps)
    beta_rows = jax.nn.sigmoid(coeffs[..., H:])
    decay_rows = -jnp.exp(decay_log) * jax.nn.softplus(coeffs[..., :H] + decay_bias)
    return (queries, key_rows, value_rows, beta_rows, decay_rows)

def head_output(readout, gate_rows, head_gain):
    scaling = lax.rsqrt(lax.optimization_barrier(jnp.mean(readout * readout, axis=-1, keepdims=True)) + norm_eps)
    gated = readout * scaling * head_gain * jax.nn.silu(gate_rows.reshape(readout.shape))
    return gated.reshape(readout.shape[:2] + (-1,))

def project(left_arr, right_arr):
    return jnp.einsum('pld,de->ple', left_arr, right_arr, precision=highest)

def layer_forward(inputs, norm_gain, qkv_weight, gate_weight, mix_weight, conv_weight, decay_log, decay_bias, head_gain, out_weight, ffn_gain, hidden_gate, hidden_up, hidden_down, segments):
    pack_count = inputs.shape[0]
    normed = low(rms_norm(inputs, norm_gain))
    mixed_rows = low_back(low(project(normed, qkv_weight)))
    gate_rows = low_back(project(normed, gate_weight))
    coeffs = low_back(project(normed, mix_weight))
    leading = jnp.zeros((pack_count, CONV - 1, mixed_rows.shape[2]), mixed_rows.dtype)
    extended = jnp.concatenate([leading, mixed_rows], axis=1)
    ext_segs = jnp.concatenate([jnp.full((pack_count, CONV - 1), -1, jnp.int32), segments], axis=1)
    pieces = front_end(extended, conv_weight, coeffs, decay_log, decay_bias, ext_segs, segments)
    zero_state = jnp.zeros((pack_count, H, DK, DV), inputs.dtype)
    first_prev = jnp.full((pack_count,), -1, jnp.int32)
    readout, _ = run_blocks(*pieces, segments, zero_state, first_prev)
    merged = low(head_output(readout, gate_rows, head_gain))
    middle = inputs + low_back(project(merged, out_weight))
    normed_ffn = low(rms_norm(middle, ffn_gain))
    gate_act = low_back(project(normed_ffn, hidden_gate))
    up_act = low_back(project(normed_ffn, hidden_up))
    hidden = low(jax.nn.silu(gate_act) * up_act)
    return middle + low_back(project(hidden, hidden_down))

def reference(inputs, segments, norm_gain, qkv_weight, gate_weight, mix_weight, conv_weight, decay_log, decay_bias, head_gain, out_weight, ffn_gain, hidden_gate, hidden_up, hidden_down, cotangent):
    floats = tuple((array.astype(jnp.float32) for array in (inputs, norm_gain, qkv_weight, gate_weight, mix_weight, conv_weight, decay_log, decay_bias, head_gain, out_weight, ffn_gain, hidden_gate, hidden_up, hidden_down)))

    def wrapped(*params):
        return layer_forward(*params, segments)
    result, pull_back = jax.vjp(wrapped, *floats)
    grads = pull_back(cotangent.astype(jnp.float32))
    return (result.astype(jnp.bfloat16), grads[0], grads[1], grads[2], grads[3], grads[4], grads[5], grads[6], grads[7], grads[8], grads[9], grads[10], grads[11], grads[12], grads[13])
```

```python
import jax
import jax.numpy as jnp
from jax import lax
from jax.sharding import PartitionSpec as P

H = 4
DK = 128
DV = 256
CONV = 4
GROUP = 64


norm_eps = 1e-06


def passed_along(value, axis, steps):
    count = lax.axis_size(axis)
    leading, last = (max(0, -steps), min(count, count - steps))
    return lax.ppermute(value, axis, [(source, source + steps) for source in range(leading, last)])


def swapped(value, axis, bit):
    return lax.ppermute(value, axis, [(i, i ^ bit) for i in range(lax.axis_size(axis))])


def up_bits(axis):
    count = lax.axis_size(axis)
    return [1 << i for i in range(count.bit_length() - 1)]


def bit_of(axis, bit):
    return (lax.axis_index(axis) // bit) % 2


def mul(spec, left, right):
    return jnp.einsum(spec, left, right, precision=lax.Precision.HIGH)


def send_quiet(value):
    return value.astype(jnp.bfloat16)


def gather_small(part):
    if lax.axis_size("fsdp") != 2:
        return lax.all_gather(part, "fsdp", axis=0, tiled=True)
    other = swapped(part, "fsdp", 1)
    low = lax.axis_index("fsdp") == 0
    return jnp.concatenate([jnp.where(low, part, other), jnp.where(low, other, part)], axis=0)


def gather_rows(part, after):
    if lax.axis_size("fsdp") != 2 or lax.axis_size("seq") % 4:
        return lax.all_gather(part, "fsdp", axis=0, tiled=True), None
    rows, cols = part.shape
    mine = lax.axis_index("seq") % 4
    fsdp_index = lax.axis_index("fsdp")
    piece = lax.dynamic_slice_in_dim(part, mine * (rows // 4), rows // 4, 0)
    if after is not None:
        piece, _ = lax.optimization_barrier((piece, after))
    first = swapped(piece, "fsdp", 1)
    second = swapped(first, "seq", 2)
    third = swapped(first, "seq", 1)
    fourth = swapped(second, "seq", 1)
    whole = jnp.concatenate([part, part], axis=0)
    base = (1 - fsdp_index) * rows
    for flip, block in ((0, first), (2, second), (1, third), (3, fourth)):
        whole = lax.dynamic_update_slice_in_dim(whole, block, base + (mine ^ flip) * (rows // 4), 0)
    return whole, first


def scatter_sum(grad_t, order):
    left = up_bits("seq")[::-1]
    current = grad_t.astype(jnp.bfloat16)
    for number, (axis, bit) in enumerate(order):
        mine = bit_of(axis, bit)
        width = current.shape[1]
        if axis == "seq":
            parts = 1 << left.index(bit)
            left.remove(bit)
            view = current.reshape(parts, 2, -1, width)
            keep = lax.dynamic_index_in_dim(view, mine, 1, False).reshape(-1, width)
            give = lax.dynamic_index_in_dim(view, 1 - mine, 1, False).reshape(-1, width)
        else:
            half = width // 2
            keep = lax.dynamic_slice_in_dim(current, mine * half, half, 1)
            give = lax.dynamic_slice_in_dim(current, (1 - mine) * half, half, 1)
        got = swapped(give, axis, bit)
        current = keep.astype(jnp.float32) + got.astype(jnp.float32)
        if number < len(order) - 1:
            current = current.astype(jnp.bfloat16)
    return jnp.transpose(current)


def scatter_orders():
    along = [("seq", bit) for bit in up_bits("seq")]
    across = [("fsdp", bit) for bit in up_bits("fsdp")[::-1]]
    near, side, far = along[:1], along[1:2], along[2:]
    return (
        near + across + side + far,
        near + side + far + across,
        near + far[:1] + across + side + far[1:],
    )


def sum_everywhere(parts):
    flat = jnp.concatenate([part.reshape(-1) for part in parts])
    for axis in ("seq", "fsdp"):
        for bit in up_bits(axis):
            flat = flat + swapped(flat, axis, bit)
    result, at = [], 0
    for part in parts:
        result.append(flat[at : at + part.size].reshape(part.shape))
        at += part.size
    return result


def unit_lower_inverse(strict):
    length = strict.shape[-1]
    rows = lax.broadcasted_iota(jnp.int32, (length, length), 0)
    cols = lax.broadcasted_iota(jnp.int32, (length, length), 1)
    result = jnp.broadcast_to(jnp.eye(length, dtype=strict.dtype), strict.shape)
    size = 1
    while size < length:
        pair = (rows // (2 * size) == cols // (2 * size)) & (rows // size > cols // size)
        corner = jnp.where(pair, strict, 0.0)
        if size == 1:
            result = result - corner
        else:
            result = result - mul("phij,phjk->phik", result, mul("phij,phjk->phik", corner, result))
        size *= 2
    return result


@jax.custom_vjp
def solve_with(inverse, strict, right_side):
    return mul("phij,phjv->phiv", inverse, right_side)


def solve_keep(inverse, strict, right_side):
    solved = mul("phij,phjv->phiv", inverse, right_side)
    return solved, (inverse, solved)


def solve_back(kept, grad):
    inverse, solved = kept
    back = mul("phji,phjv->phiv", inverse, grad)
    return jnp.zeros_like(inverse), -mul("phiv,phjv->phij", back, solved), back


solve_with.defvjp(solve_keep, solve_back)


def rms_norm(values, gain_vec):
    return (
        values * lax.rsqrt(jnp.mean(values * values, axis=-1, keepdims=True) + norm_eps) * gain_vec
    )


def spread_terms(key_heads, beta_heads, decay_rows, segments, first_prev):
    length = segments.shape[1]
    row_index = lax.broadcasted_iota(jnp.int32, (length, length), 0)
    col_index = lax.broadcasted_iota(jnp.int32, (length, length), 1)
    totals = jnp.swapaxes(jnp.cumsum(decay_rows, axis=1), 1, 2)
    same_doc = ((segments[:, :, None] == segments[:, None, :]) & (col_index <= row_index)[None])[
        :, None
    ]
    spread = totals[:, :, :, None] - totals[:, :, None, :]
    weight = jnp.where(same_doc, jnp.exp(jnp.where(same_doc, spread, 0.0)), 0.0)
    keep_prev = (segments == first_prev[:, None]).astype(totals.dtype)
    start_gain = jnp.exp(totals) * keep_prev[:, None, :]
    key_inner = mul("phik,phjk->phij", key_heads, key_heads)
    strict = jnp.where(col_index < row_index, weight * key_inner * beta_heads[:, :, None, :], 0.0)
    tail = key_heads * (weight[:, :, -1, :] * beta_heads)[..., None]
    return weight, start_gain, strict, tail


def to_heads(pieces):
    queries, key_rows, value_rows, beta_rows, decay_rows = pieces
    heads = [jnp.swapaxes(part, 1, 2) for part in (queries, key_rows, value_rows, beta_rows)]
    return (*heads, decay_rows)


def local_maps(pieces, segments, first_prev):
    _, keys, values, betas, decay_rows = to_heads(pieces)
    _, start_gain, strict, tail = spread_terms(keys, betas, decay_rows, segments, first_prev)
    inverse = unit_lower_inverse(strict)
    right_side = jnp.concatenate([start_gain[..., None] * keys, values], axis=-1)
    solved = mul("phij,phjv->phiv", inverse, right_side)
    change = mul("phck,phcv->phkv", tail, solved)
    identity = jnp.eye(DK, dtype=keys.dtype)
    carry_map = start_gain[:, :, -1, None, None] * identity - change[..., :DK]
    return inverse, carry_map, change[..., DK:]


def run_local(pieces, state_in, inverse, segments, first_prev):
    queries, keys, values, betas, decay_rows = to_heads(pieces)
    weight, start_gain, strict, tail = spread_terms(keys, betas, decay_rows, segments, first_prev)
    gains = start_gain[..., None]
    from_keys = mul("phck,phkv->phcv", gains * keys, state_in)
    solved = solve_with(inverse, strict, values - from_keys)
    scores = weight * mul("phik,phjk->phij", queries, keys) * betas[:, :, None, :]
    readout = mul("phck,phkv->phcv", gains * queries, state_in)
    readout = readout + mul("phij,phjv->phiv", scores, solved)
    state_out = start_gain[:, :, -1, None, None] * state_in
    state_out = state_out + mul("phck,phcv->phkv", tail, solved)
    return jnp.swapaxes(readout, 1, 2), state_out


def state_before(carry_map, carry_add):
    bits = up_bits("seq")
    before_map = jnp.broadcast_to(jnp.eye(DK, dtype=carry_map.dtype), carry_map.shape)
    after_map = before_map
    before = jnp.zeros_like(carry_add)
    kept = []
    for bit in bits:
        later = bit_of("seq", bit) == 1
        last = bit == bits[-1]
        other_add = swapped(send_quiet(carry_add), "seq", bit).astype(jnp.float32)
        if last:
            before = jnp.where(
                later, mul("phij,phjk->phik", before_map, other_add) + before, before
            )
            kept.append((after_map, None))
            break
        other_map = swapped(send_quiet(carry_map), "seq", bit).astype(jnp.float32)
        both = mul(
            "phij,phjk->phik", before_map, jnp.concatenate([other_map, other_add], axis=-1)
        )
        first_map = jnp.where(later, other_map, carry_map)
        first_add = jnp.where(later, other_add, carry_add)
        second_map = jnp.where(later, carry_map, other_map)
        second_add = jnp.where(later, carry_add, other_add)
        kept.append((after_map, first_map))
        after_map = jnp.where(later, after_map, mul("phij,phjk->phik", other_map, after_map))
        before = jnp.where(later, both[..., DK:] + before, before)
        before_map = jnp.where(later, both[..., :DK], before_map)
        total = mul(
            "phij,phjk->phik", second_map, jnp.concatenate([first_map, first_add], axis=-1)
        )
        carry_map, carry_add = total[..., :DK], total[..., DK:] + second_add
    return before, kept


def adjoint_after(local_term, kept):
    bits = up_bits("seq")
    after = jnp.zeros_like(local_term)
    total = local_term
    for bit, (after_map, first_map) in zip(bits, kept):
        later = bit_of("seq", bit) == 1
        other = swapped(send_quiet(total), "seq", bit).astype(jnp.float32)
        after = jnp.where(later, after, mul("phji,phjk->phik", after_map, other) + after)
        if first_map is not None:
            second = jnp.where(later, total, other)
            first = jnp.where(later, other, total)
            total = mul("phji,phjk->phik", first_map, second) + first
    return after


def front_end(extended, conv_weight, coeffs, decay_log, decay_bias, ext_segs, segments):
    length_all = segments.shape[1]
    summed = jnp.zeros(extended.shape[:1] + (length_all,) + extended.shape[2:], extended.dtype)
    for offset in range(CONV):
        window = extended[:, offset : offset + length_all]
        same_seg = (ext_segs[:, offset : offset + length_all] == segments)[..., None]
        summed = summed + conv_weight[offset] * jnp.where(same_seg, window, 0.0)
    activated = jax.nn.silu(summed)
    lead_shape = activated.shape[:2]
    key_span = H * DK
    queries = activated[..., :key_span].reshape(lead_shape + (H, DK))
    key_rows = activated[..., key_span : 2 * key_span].reshape(lead_shape + (H, DK))
    value_rows = activated[..., 2 * key_span :].reshape(lead_shape + (H, DV))
    queries = (
        queries
        * lax.rsqrt(jnp.sum(queries * queries, axis=-1, keepdims=True) + norm_eps)
        * DK ** (-0.5)
    )
    key_rows = key_rows * lax.rsqrt(jnp.sum(key_rows * key_rows, axis=-1, keepdims=True) + norm_eps)
    beta_rows = jax.nn.sigmoid(coeffs[..., H:])
    decay_rows = -jnp.exp(decay_log) * jax.nn.softplus(coeffs[..., :H] + decay_bias)
    return (queries, key_rows, value_rows, beta_rows, decay_rows)


def head_output(readout, gate_rows, head_gain):
    scaling = lax.rsqrt(jnp.mean(readout * readout, axis=-1, keepdims=True) + norm_eps)
    gated = readout * scaling * head_gain * jax.nn.silu(gate_rows.reshape(readout.shape))
    return gated.reshape(readout.shape[:2] + (-1,))


def own_rows(whole, fsdp_index, part_count):
    row_count = whole.shape[0] // part_count
    return lax.dynamic_slice_in_dim(whole, fsdp_index * row_count, row_count, 0)


def per_device(
    inputs,
    segments,
    norm_gain,
    qkv_weight,
    gate_weight,
    mix_weight,
    conv_weight,
    decay_log,
    decay_bias,
    head_gain,
    out_weight,
    ffn_gain,
    hidden_gate,
    hidden_up,
    hidden_down,
    cotangent,
):
    wide = qkv_weight.shape[1]
    value_span = gate_weight.shape[1]
    half_ffn = hidden_gate.shape[1]
    pad = (-mix_weight.shape[1]) % 128
    first_weights, done = gather_rows(
        jnp.concatenate([qkv_weight, gate_weight, jnp.pad(mix_weight, ((0, 0), (0, pad)))], axis=1),
        None,
    )
    out_full, done = gather_rows(out_weight, done)
    ffn_weights, done = gather_rows(jnp.concatenate([hidden_gate, hidden_up], axis=1), done)
    down_ffn, done = gather_rows(hidden_down, done)
    norm_full, head_full, ffn_full = (
        gather_small(norm_gain),
        gather_small(head_gain),
        gather_small(ffn_gain),
    )
    taps_full = jnp.transpose(gather_small(conv_weight)).astype(jnp.float32)
    source = inputs.astype(jnp.float32)
    normed_f, pull_first = jax.vjp(rms_norm, source, norm_full.astype(jnp.float32))
    normed = normed_f.astype(jnp.bfloat16)
    projected = jnp.einsum(
        "ptd,de->pte", normed, first_weights, preferred_element_type=jnp.float32
    )
    mixed_rows = projected[..., :wide].astype(jnp.bfloat16)
    gate_rows = projected[..., wide : wide + value_span]
    coeffs = projected[..., wide + value_span : wide + value_span + 2 * H]
    rim_size = CONV - 1
    rim_values, rim_marks = passed_along(
        (mixed_rows[:, -rim_size:], segments[:, -rim_size:].astype(jnp.bfloat16)), "seq", 1
    )
    extended = jnp.concatenate([rim_values, mixed_rows], axis=1).astype(jnp.float32)
    ext_segs = jnp.concatenate([rim_marks.astype(jnp.int32), segments], axis=1)
    first_prev = ext_segs[:, rim_size - 1]

    def front_local(ext_rows, taps, coeff_rows, rate_log, rate_bias):
        return front_end(ext_rows, taps, coeff_rows, rate_log, rate_bias, ext_segs, segments)

    pieces, pull_front = jax.vjp(
        front_local, extended, taps_full, coeffs, decay_log, decay_bias
    )
    inverse, carry_map, carry_add = local_maps(pieces, segments, first_prev)
    state_in, kept_maps = state_before(carry_map, carry_add)

    def recurrence(parts, state_start):
        return run_local(parts, state_start, inverse, segments, first_prev)

    (readout, state_out), pull_rec = jax.vjp(recurrence, pieces, state_in)
    merged_f, pull_head = jax.vjp(head_output, readout, gate_rows, head_full.astype(jnp.float32))
    merged = merged_f.astype(jnp.bfloat16)
    branch = jnp.einsum("pte,ed->ptd", merged, out_full, preferred_element_type=jnp.float32)
    middle = source + branch
    normed_ffn_f, pull_second = jax.vjp(rms_norm, middle, ffn_full.astype(jnp.float32))
    normed_ffn = normed_ffn_f.astype(jnp.bfloat16)
    acts = jnp.einsum("ptd,df->ptf", normed_ffn, ffn_weights, preferred_element_type=jnp.float32)
    gate_act, up_act = acts[..., :half_ffn], acts[..., half_ffn:]
    sigmoid_gate = jax.nn.sigmoid(gate_act)
    swish_gate = gate_act * sigmoid_gate
    hidden = (swish_gate * up_act).astype(jnp.bfloat16)
    ffn_out = jnp.einsum("ptf,fd->ptd", hidden, down_ffn, preferred_element_type=jnp.float32)
    outputs = (middle + ffn_out).astype(jnp.bfloat16)
    back_hidden = jnp.einsum("ptd,fd->ptf", cotangent, down_ffn, preferred_element_type=jnp.float32)
    back_gate = (back_hidden * up_act * (sigmoid_gate + swish_gate * (1.0 - sigmoid_gate))).astype(
        jnp.bfloat16
    )
    back_up = (back_hidden * swish_gate).astype(jnp.bfloat16)
    low_first, high_first, mid_first = scatter_orders()
    grad_down = jnp.einsum("ptd,ptf->df", cotangent, hidden, preferred_element_type=jnp.float32)
    owned_down = scatter_sum(grad_down, mid_first)
    grad_gate_ffn = jnp.einsum(
        "ptf,ptd->fd", back_gate, normed_ffn, preferred_element_type=jnp.float32
    )
    owned_gate_ffn = scatter_sum(grad_gate_ffn, low_first)
    grad_up_ffn = jnp.einsum("ptf,ptd->fd", back_up, normed_ffn, preferred_element_type=jnp.float32)
    owned_up_ffn = scatter_sum(grad_up_ffn, high_first)
    back_normed_ffn = jnp.einsum(
        "ptf,df->ptd",
        jnp.concatenate([back_gate, back_up], axis=-1),
        ffn_weights,
        preferred_element_type=jnp.float32,
    )
    middle_part, grad_ffn_full = pull_second(back_normed_ffn)
    back_middle = cotangent.astype(jnp.float32) + middle_part
    back_branch = back_middle.astype(jnp.bfloat16)
    grad_out = jnp.einsum("ptd,pte->de", back_branch, merged, preferred_element_type=jnp.float32)
    owned_out = scatter_sum(grad_out, high_first)
    back_merged = jnp.einsum(
        "ptd,ed->pte", back_branch, out_full, preferred_element_type=jnp.float32
    )
    back_readout, back_gates_f, grad_head_full = pull_head(back_merged)
    _, local_term = pull_rec((back_readout, jnp.zeros_like(state_out)))
    later_grad = adjoint_after(local_term, kept_maps)
    back_pieces, _ = pull_rec((back_readout, later_grad))
    back_extended, grad_taps, back_coeffs_f, grad_decay_log, grad_decay_bias = pull_front(
        back_pieces
    )
    back_rim = passed_along(back_extended[:, :rim_size], "seq", -1)
    tokens_here = segments.shape[1]
    back_mixed = (
        back_extended[:, rim_size:]
        + jnp.pad(back_rim, ((0, 0), (tokens_here - rim_size, 0), (0, 0)))
    ).astype(jnp.bfloat16)
    back_gates = back_gates_f.astype(jnp.bfloat16)
    back_coeffs = back_coeffs_f.astype(jnp.bfloat16)
    grad_qkv = jnp.einsum("pte,ptd->ed", back_mixed, normed, preferred_element_type=jnp.float32)
    grad_gate = jnp.einsum("pte,ptd->ed", back_gates, normed, preferred_element_type=jnp.float32)
    grad_mix = jnp.einsum("pte,ptd->ed", back_coeffs, normed, preferred_element_type=jnp.float32)
    owned_gate = scatter_sum(grad_gate, mid_first)
    owned_qkv = scatter_sum(grad_qkv, low_first)
    back_all = jnp.concatenate(
        [back_mixed, back_gates, jnp.pad(back_coeffs, ((0, 0), (0, 0), (0, pad)))], axis=-1
    )
    back_normed = jnp.einsum(
        "pte,de->ptd", back_all, first_weights, preferred_element_type=jnp.float32
    )
    source_part, grad_norm_full = pull_first(back_normed)
    input_grad = back_middle + source_part
    fsdp_index = lax.axis_index("fsdp")
    fsdp_count = lax.axis_size("fsdp")
    small_sums = sum_everywhere(
        (
            grad_norm_full,
            grad_head_full,
            grad_ffn_full,
            grad_taps,
            grad_decay_log,
            grad_decay_bias,
            grad_mix,
        )
    )
    taps_own = own_rows(jnp.transpose(small_sums[3]), fsdp_index, fsdp_count)
    mix_own = own_rows(jnp.transpose(small_sums[6]), fsdp_index, fsdp_count)
    return (
        outputs,
        input_grad,
        own_rows(small_sums[0], fsdp_index, fsdp_count),
        owned_qkv,
        owned_gate,
        mix_own,
        taps_own,
        small_sums[4],
        small_sums[5],
        own_rows(small_sums[1], fsdp_index, fsdp_count),
        owned_out,
        own_rows(small_sums[2], fsdp_index, fsdp_count),
        owned_gate_ffn,
        owned_up_ffn,
        owned_down,
    )


def solution(mesh):
    in_specs = (
        P("fsdp", "seq", None),
        P("fsdp", "seq"),
        P("fsdp"),
        P("fsdp", None),
        P("fsdp", None),
        P("fsdp", None),
        P("fsdp", None),
        P(),
        P(),
        P("fsdp"),
        P("fsdp", None),
        P("fsdp"),
        P("fsdp", None),
        P("fsdp", None),
        P("fsdp", None),
        P("fsdp", "seq", None),
    )
    out_specs = (
        P("fsdp", "seq", None),
        P("fsdp", "seq", None),
        P("fsdp"),
        P("fsdp", "seq"),
        P("fsdp", "seq"),
        P("fsdp", None),
        P("fsdp", None),
        P(),
        P(),
        P("fsdp"),
        P("fsdp", "seq"),
        P("fsdp"),
        P("fsdp", "seq"),
        P("fsdp", "seq"),
        P("fsdp", "seq"),
    )
    return jax.shard_map(
        per_device, mesh=mesh, in_specs=in_specs, out_specs=out_specs, check_vma=False
    )
```

```python
import jax
import jax.numpy as jnp
from jax import lax
from jax.sharding import PartitionSpec as P

H = 4
DK = 128
DV = 256
CONV = 4
GROUP = 64


norm_eps = 1e-06


def passed_along(value, axis, steps):
    count = lax.axis_size(axis)
    leading, last = (max(0, -steps), min(count, count - steps))
    return lax.ppermute(value, axis, [(source, source + steps) for source in range(leading, last)])


def swapped(value, axis, bit):
    return lax.ppermute(value, axis, [(i, i ^ bit) for i in range(lax.axis_size(axis))])


def up_bits(axis):
    count = lax.axis_size(axis)
    return [1 << i for i in range(count.bit_length() - 1)]


def bit_of(axis, bit):
    return (lax.axis_index(axis) // bit) % 2


def mul(spec, left, right):
    return jnp.einsum(spec, left, right, precision=lax.Precision.HIGH)


def send_quiet(value):
    return value.astype(jnp.bfloat16)


def gather_small(part):
    if lax.axis_size("fsdp") != 2:
        return lax.all_gather(part, "fsdp", axis=0, tiled=True)
    other = swapped(part, "fsdp", 1)
    low = lax.axis_index("fsdp") == 0
    return jnp.concatenate([jnp.where(low, part, other), jnp.where(low, other, part)], axis=0)


def gather_rows(parts, after):
    if lax.axis_size("fsdp") != 2 or lax.axis_size("seq") % 4:
        return [lax.all_gather(part, "fsdp", axis=0, tiled=True) for part in parts], after
    rows, cols = parts[0].shape
    mine = lax.axis_index("seq") % 4
    quarter = rows // 4
    piece = jnp.stack(
        [lax.dynamic_slice_in_dim(part, mine * quarter, quarter, 0) for part in parts]
    )
    if after is not None:
        piece, _ = lax.optimization_barrier((piece, after))
    first = swapped(piece, "fsdp", 1)
    second = swapped(first, "seq", 2)
    third = swapped(first, "seq", 1)
    fourth = swapped(second, "seq", 1)
    base = (1 - lax.axis_index("fsdp")) * rows
    wholes = []
    for number, part in enumerate(parts):
        whole = jnp.broadcast_to(part[None], (2, rows, cols)).reshape(2 * rows, cols)
        for flip, block in ((0, first), (2, second), (1, third), (3, fourth)):
            whole = lax.dynamic_update_slice_in_dim(
                whole, block[number], base + (mine ^ flip) * quarter, 0
            )
        wholes.append(whole)
    return wholes, first


class Scattered:
    def __init__(self, grad_t, order):
        self.current = grad_t.astype(jnp.bfloat16)
        self.left = up_bits("seq")[::-1]
        self.order = list(order)

    def step(self):
        axis, bit = self.order.pop(0)
        mine = bit_of(axis, bit)
        current = self.current
        lead, width = current.shape[:-2], current.shape[-1]
        if axis == "seq":
            parts = 1 << self.left.index(bit)
            self.left.remove(bit)
            at = len(lead) + 1
            view = current.reshape(lead + (parts, 2, -1, width))
            keep = lax.dynamic_index_in_dim(view, mine, at, False).reshape(lead + (-1, width))
            give = lax.dynamic_index_in_dim(view, 1 - mine, at, False).reshape(lead + (-1, width))
        else:
            half, at = width // 2, len(lead) + 1
            keep = lax.dynamic_slice_in_dim(current, mine * half, half, at)
            give = lax.dynamic_slice_in_dim(current, (1 - mine) * half, half, at)
        got = swapped(give, axis, bit)
        self.current = keep.astype(jnp.float32) + got.astype(jnp.float32)
        if self.order:
            self.current = self.current.astype(jnp.bfloat16)

    def finish(self):
        while self.order:
            self.step()
        return jnp.swapaxes(self.current, -1, -2)


def tied(value, sums):
    value, currents = lax.optimization_barrier((value, [item.current for item in sums]))
    for item, current in zip(sums, currents):
        item.current = current
    return value


def scatter_orders():
    along = [("seq", bit) for bit in up_bits("seq")]
    across = [("fsdp", bit) for bit in up_bits("fsdp")[::-1]]
    near, side, far = along[:1], along[1:2], along[2:]
    return (
        near + across + side + far,
        near + side + far + across,
        near + far[:1] + across + side + far[1:],
    )


def sum_everywhere(parts, beside):
    flat = jnp.concatenate([part.reshape(-1) for part in parts])
    for axis, bits in (("seq", up_bits("seq")), ("fsdp", up_bits("fsdp"))):
        for bit in bits:
            flat = tied(flat, [beside])
            if beside.order:
                beside.step()
            flat = flat + swapped(flat, axis, bit)
    result, at = [], 0
    for part in parts:
        result.append(flat[at : at + part.size].reshape(part.shape))
        at += part.size
    return result


def unit_lower_inverse(strict):
    length = strict.shape[-1]
    rows = lax.broadcasted_iota(jnp.int32, (length, length), 0)
    cols = lax.broadcasted_iota(jnp.int32, (length, length), 1)
    result = jnp.broadcast_to(jnp.eye(length, dtype=strict.dtype), strict.shape)
    size = 1
    while size < length:
        pair = (rows // (2 * size) == cols // (2 * size)) & (rows // size > cols // size)
        corner = jnp.where(pair, strict, 0.0)
        if size == 1:
            result = result - corner
        else:
            result = result - mul("phij,phjk->phik", result, mul("phij,phjk->phik", corner, result))
        size *= 2
    return result


@jax.custom_vjp
def solve_with(inverse, strict, right_side):
    return mul("phij,phjv->phiv", inverse, right_side)


def solve_keep(inverse, strict, right_side):
    solved = mul("phij,phjv->phiv", inverse, right_side)
    return solved, (inverse, solved)


def solve_back(kept, grad):
    inverse, solved = kept
    back = mul("phji,phjv->phiv", inverse, grad)
    return jnp.zeros_like(inverse), -mul("phiv,phjv->phij", back, solved), back


solve_with.defvjp(solve_keep, solve_back)


def rms_norm(values, gain_vec):
    return (
        values * lax.rsqrt(jnp.mean(values * values, axis=-1, keepdims=True) + norm_eps) * gain_vec
    )


def spread_terms(key_heads, beta_heads, decay_rows, segments, first_prev):
    length = segments.shape[1]
    row_index = lax.broadcasted_iota(jnp.int32, (length, length), 0)
    col_index = lax.broadcasted_iota(jnp.int32, (length, length), 1)
    totals = jnp.swapaxes(jnp.cumsum(decay_rows, axis=1), 1, 2)
    same_doc = ((segments[:, :, None] == segments[:, None, :]) & (col_index <= row_index)[None])[
        :, None
    ]
    spread = totals[:, :, :, None] - totals[:, :, None, :]
    weight = jnp.where(same_doc, jnp.exp(jnp.where(same_doc, spread, 0.0)), 0.0)
    keep_prev = (segments == first_prev[:, None]).astype(totals.dtype)
    start_gain = jnp.exp(totals) * keep_prev[:, None, :]
    key_inner = mul("phik,phjk->phij", key_heads, key_heads)
    strict = jnp.where(col_index < row_index, weight * key_inner * beta_heads[:, :, None, :], 0.0)
    tail = key_heads * (weight[:, :, -1, :] * beta_heads)[..., None]
    return weight, start_gain, strict, tail


def to_heads(pieces):
    queries, key_rows, value_rows, beta_rows, decay_rows = pieces
    heads = [jnp.swapaxes(part, 1, 2) for part in (queries, key_rows, value_rows, beta_rows)]
    return (*heads, decay_rows)


def local_maps(pieces, segments, first_prev):
    _, keys, values, betas, decay_rows = to_heads(pieces)
    _, start_gain, strict, tail = spread_terms(keys, betas, decay_rows, segments, first_prev)
    inverse = unit_lower_inverse(strict)
    right_side = jnp.concatenate([start_gain[..., None] * keys, values], axis=-1)
    solved = mul("phij,phjv->phiv", inverse, right_side)
    change = mul("phck,phcv->phkv", tail, solved)
    identity = jnp.eye(DK, dtype=keys.dtype)
    carry_map = start_gain[:, :, -1, None, None] * identity - change[..., :DK]
    return inverse, carry_map, change[..., DK:]


def run_local(pieces, state_in, inverse, segments, first_prev):
    queries, keys, values, betas, decay_rows = to_heads(pieces)
    weight, start_gain, strict, tail = spread_terms(keys, betas, decay_rows, segments, first_prev)
    gains = start_gain[..., None]
    from_keys = mul("phck,phkv->phcv", gains * keys, state_in)
    solved = solve_with(inverse, strict, values - from_keys)
    scores = weight * mul("phik,phjk->phij", queries, keys) * betas[:, :, None, :]
    readout = mul("phck,phkv->phcv", gains * queries, state_in)
    readout = readout + mul("phij,phjv->phiv", scores, solved)
    state_out = start_gain[:, :, -1, None, None] * state_in
    state_out = state_out + mul("phck,phcv->phkv", tail, solved)
    return jnp.swapaxes(readout, 1, 2), state_out


def state_before(carry_map, carry_add):
    bits = up_bits("seq")
    before_map = jnp.broadcast_to(jnp.eye(DK, dtype=carry_map.dtype), carry_map.shape)
    after_map = before_map
    before = jnp.zeros_like(carry_add)
    kept = []
    for bit in bits:
        later = bit_of("seq", bit) == 1
        last = bit == bits[-1]
        other_add = swapped(send_quiet(carry_add), "seq", bit).astype(jnp.float32)
        if last:
            before = jnp.where(
                later, mul("phij,phjk->phik", before_map, other_add) + before, before
            )
            kept.append((after_map, None))
            break
        other_map = swapped(send_quiet(carry_map), "seq", bit).astype(jnp.float32)
        both = mul(
            "phij,phjk->phik", before_map, jnp.concatenate([other_map, other_add], axis=-1)
        )
        first_map = jnp.where(later, other_map, carry_map)
        first_add = jnp.where(later, other_add, carry_add)
        second_map = jnp.where(later, carry_map, other_map)
        second_add = jnp.where(later, carry_add, other_add)
        kept.append((after_map, first_map))
        after_map = jnp.where(later, after_map, mul("phij,phjk->phik", other_map, after_map))
        before = jnp.where(later, both[..., DK:] + before, before)
        before_map = jnp.where(later, both[..., :DK], before_map)
        total = mul(
            "phij,phjk->phik", second_map, jnp.concatenate([first_map, first_add], axis=-1)
        )
        carry_map, carry_add = total[..., :DK], total[..., DK:] + second_add
    return before, kept


def adjoint_after(local_term, kept):
    bits = up_bits("seq")
    after = jnp.zeros_like(local_term)
    total = local_term
    for bit, (after_map, first_map) in zip(bits, kept):
        later = bit_of("seq", bit) == 1
        other = swapped(send_quiet(total), "seq", bit).astype(jnp.float32)
        after = jnp.where(later, after, mul("phji,phjk->phik", after_map, other) + after)
        if first_map is not None:
            second = jnp.where(later, total, other)
            first = jnp.where(later, other, total)
            total = mul("phji,phjk->phik", first_map, second) + first
    return after


def front_end(extended, conv_weight, coeffs, decay_log, decay_bias, ext_segs, segments):
    length_all = segments.shape[1]
    summed = jnp.zeros(extended.shape[:1] + (length_all,) + extended.shape[2:], extended.dtype)
    for offset in range(CONV):
        window = extended[:, offset : offset + length_all]
        same_seg = (ext_segs[:, offset : offset + length_all] == segments)[..., None]
        summed = summed + conv_weight[offset] * jnp.where(same_seg, window, 0.0)
    activated = jax.nn.silu(summed)
    lead_shape = activated.shape[:2]
    key_span = H * DK
    queries = activated[..., :key_span].reshape(lead_shape + (H, DK))
    key_rows = activated[..., key_span : 2 * key_span].reshape(lead_shape + (H, DK))
    value_rows = activated[..., 2 * key_span :].reshape(lead_shape + (H, DV))
    queries = (
        queries
        * lax.rsqrt(jnp.sum(queries * queries, axis=-1, keepdims=True) + norm_eps)
        * DK ** (-0.5)
    )
    key_rows = key_rows * lax.rsqrt(jnp.sum(key_rows * key_rows, axis=-1, keepdims=True) + norm_eps)
    beta_rows = jax.nn.sigmoid(coeffs[..., H:])
    decay_rows = -jnp.exp(decay_log) * jax.nn.softplus(coeffs[..., :H] + decay_bias)
    return (queries, key_rows, value_rows, beta_rows, decay_rows)


def head_output(readout, gate_rows, head_gain):
    scaling = lax.rsqrt(jnp.mean(readout * readout, axis=-1, keepdims=True) + norm_eps)
    gated = readout * scaling * head_gain * jax.nn.silu(gate_rows.reshape(readout.shape))
    return gated.reshape(readout.shape[:2] + (-1,))


def own_rows(whole, fsdp_index, part_count):
    row_count = whole.shape[0] // part_count
    return lax.dynamic_slice_in_dim(whole, fsdp_index * row_count, row_count, 0)


def per_device(
    inputs,
    segments,
    norm_gain,
    qkv_weight,
    gate_weight,
    mix_weight,
    conv_weight,
    decay_log,
    decay_bias,
    head_gain,
    out_weight,
    ffn_gain,
    hidden_gate,
    hidden_up,
    hidden_down,
    cotangent,
):
    (qkv_full,), done = gather_rows([qkv_weight], None)
    norm_full, mix_full = gather_small(norm_gain), gather_small(mix_weight)
    taps_full = jnp.transpose(gather_small(conv_weight)).astype(jnp.float32)
    (gate_full, out_full), _ = gather_rows([gate_weight, out_weight], done)
    (gate_ffn, up_ffn), _ = gather_rows([hidden_gate, hidden_up], done)
    (down_ffn,), _ = gather_rows([hidden_down], done)
    head_full, ffn_full = gather_small(head_gain), gather_small(ffn_gain)
    source = inputs.astype(jnp.float32)
    normed_f, pull_first = jax.vjp(rms_norm, source, norm_full.astype(jnp.float32))
    normed = normed_f.astype(jnp.bfloat16)
    mixed_rows = jnp.einsum(
        "ptd,de->pte", normed, qkv_full, preferred_element_type=jnp.float32
    ).astype(jnp.bfloat16)
    gate_rows = jnp.einsum("ptd,de->pte", normed, gate_full, preferred_element_type=jnp.float32)
    coeffs = jnp.einsum("ptd,de->pte", normed, mix_full, preferred_element_type=jnp.float32)
    rim_size = CONV - 1
    rim_values, rim_marks = passed_along(
        (mixed_rows[:, -rim_size:], segments[:, -rim_size:].astype(jnp.bfloat16)), "seq", 1
    )
    extended = jnp.concatenate([rim_values, mixed_rows], axis=1).astype(jnp.float32)
    ext_segs = jnp.concatenate([rim_marks.astype(jnp.int32), segments], axis=1)
    first_prev = ext_segs[:, rim_size - 1]

    def front_local(ext_rows, taps, coeff_rows, rate_log, rate_bias):
        return front_end(ext_rows, taps, coeff_rows, rate_log, rate_bias, ext_segs, segments)

    pieces, pull_front = jax.vjp(
        front_local, extended, taps_full, coeffs, decay_log, decay_bias
    )
    inverse, carry_map, carry_add = local_maps(pieces, segments, first_prev)
    state_in, kept_maps = state_before(carry_map, carry_add)

    def recurrence(parts, state_start):
        return run_local(parts, state_start, inverse, segments, first_prev)

    (readout, state_out), pull_rec = jax.vjp(recurrence, pieces, state_in)
    merged_f, pull_head = jax.vjp(head_output, readout, gate_rows, head_full.astype(jnp.float32))
    merged = merged_f.astype(jnp.bfloat16)
    branch = jnp.einsum("pte,ed->ptd", merged, out_full, preferred_element_type=jnp.float32)
    middle = source + branch
    normed_ffn_f, pull_second = jax.vjp(rms_norm, middle, ffn_full.astype(jnp.float32))
    normed_ffn = normed_ffn_f.astype(jnp.bfloat16)
    gate_act = jnp.einsum("ptd,df->ptf", normed_ffn, gate_ffn, preferred_element_type=jnp.float32)
    up_act = jnp.einsum("ptd,df->ptf", normed_ffn, up_ffn, preferred_element_type=jnp.float32)
    sigmoid_gate = jax.nn.sigmoid(gate_act)
    swish_gate = gate_act * sigmoid_gate
    hidden = (swish_gate * up_act).astype(jnp.bfloat16)
    ffn_out = jnp.einsum("ptf,fd->ptd", hidden, down_ffn, preferred_element_type=jnp.float32)
    outputs = (middle + ffn_out).astype(jnp.bfloat16)
    back_hidden = jnp.einsum("ptd,fd->ptf", cotangent, down_ffn, preferred_element_type=jnp.float32)
    back_gate = (back_hidden * up_act * (sigmoid_gate + swish_gate * (1.0 - sigmoid_gate))).astype(
        jnp.bfloat16
    )
    back_up = (back_hidden * swish_gate).astype(jnp.bfloat16)
    low_first, high_first, mid_first = scatter_orders()
    grad_down = jnp.einsum("ptd,ptf->df", cotangent, hidden, preferred_element_type=jnp.float32)
    grad_gate_ffn = jnp.einsum(
        "ptf,ptd->fd", back_gate, normed_ffn, preferred_element_type=jnp.float32
    )
    grad_up_ffn = jnp.einsum("ptf,ptd->fd", back_up, normed_ffn, preferred_element_type=jnp.float32)
    early = [
        Scattered(grad_down, mid_first),
        Scattered(grad_gate_ffn, low_first),
        Scattered(grad_up_ffn, high_first),
    ]
    for item in early:
        item.step()
    back_normed_ffn = jnp.einsum(
        "ptf,df->ptd", back_gate, gate_ffn, preferred_element_type=jnp.float32
    )
    back_normed_ffn = back_normed_ffn + jnp.einsum(
        "ptf,df->ptd", back_up, up_ffn, preferred_element_type=jnp.float32
    )
    middle_part, grad_ffn_full = pull_second(back_normed_ffn)
    back_middle = cotangent.astype(jnp.float32) + middle_part
    back_branch = back_middle.astype(jnp.bfloat16)
    grad_out = jnp.einsum("ptd,pte->de", back_branch, merged, preferred_element_type=jnp.float32)
    back_merged = jnp.einsum(
        "ptd,ed->pte", back_branch, out_full, preferred_element_type=jnp.float32
    )
    back_readout, back_gates_f, grad_head_full = pull_head(back_merged)
    _, local_term = pull_rec((back_readout, jnp.zeros_like(state_out)))
    later_grad = tied(adjoint_after(local_term, kept_maps), early)
    back_gates = back_gates_f.astype(jnp.bfloat16)
    grad_gate = jnp.einsum("pte,ptd->ed", back_gates, normed, preferred_element_type=jnp.float32)
    early.append(Scattered(jnp.stack([grad_out, grad_gate]), low_first))
    for item in early:
        item.step()
    back_pieces, _ = pull_rec((back_readout, later_grad))
    back_pieces = tied(back_pieces, early)
    for item in early:
        item.step()
    back_extended, grad_taps, back_coeffs_f, grad_decay_log, grad_decay_bias = pull_front(
        back_pieces
    )
    back_extended = tied(back_extended, early)
    for item in early:
        item.step()
    back_rim = passed_along(back_extended[:, :rim_size], "seq", -1)
    tokens_here = segments.shape[1]
    back_mixed = (
        back_extended[:, rim_size:]
        + jnp.pad(back_rim, ((0, 0), (tokens_here - rim_size, 0), (0, 0)))
    ).astype(jnp.bfloat16)
    back_coeffs = back_coeffs_f.astype(jnp.bfloat16)
    grad_qkv = jnp.einsum("pte,ptd->ed", back_mixed, normed, preferred_element_type=jnp.float32)
    late = Scattered(grad_qkv, low_first)
    late.step()
    grad_mix = jnp.einsum("pte,ptd->ed", back_coeffs, normed, preferred_element_type=jnp.float32)
    back_normed = jnp.einsum(
        "pte,de->ptd", back_mixed, qkv_full, preferred_element_type=jnp.float32
    )
    back_normed = back_normed + jnp.einsum(
        "pte,de->ptd", back_gates, gate_full, preferred_element_type=jnp.float32
    )
    back_normed = back_normed + jnp.einsum(
        "pte,de->ptd", back_coeffs, mix_full, preferred_element_type=jnp.float32
    )
    source_part, grad_norm_full = pull_first(back_normed)
    input_grad = back_middle + source_part
    fsdp_index = lax.axis_index("fsdp")
    fsdp_count = lax.axis_size("fsdp")
    owned_down, owned_gate_ffn, owned_up_ffn, owned_pair = [item.finish() for item in early]
    owned_out, owned_gate = owned_pair[0], owned_pair[1]
    small_sums = sum_everywhere(
        (
            grad_norm_full,
            grad_head_full,
            grad_ffn_full,
            grad_taps,
            grad_decay_log,
            grad_decay_bias,
            grad_mix,
        ),
        late,
    )
    owned_qkv = late.finish()
    taps_own = own_rows(jnp.transpose(small_sums[3]), fsdp_index, fsdp_count)
    mix_own = own_rows(jnp.transpose(small_sums[6]), fsdp_index, fsdp_count)
    return (
        outputs,
        input_grad,
        own_rows(small_sums[0], fsdp_index, fsdp_count),
        owned_qkv,
        owned_gate,
        mix_own,
        taps_own,
        small_sums[4],
        small_sums[5],
        own_rows(small_sums[1], fsdp_index, fsdp_count),
        owned_out,
        own_rows(small_sums[2], fsdp_index, fsdp_count),
        owned_gate_ffn,
        owned_up_ffn,
        owned_down,
    )


def solution(mesh):
    in_specs = (
        P("fsdp", "seq", None),
        P("fsdp", "seq"),
        P("fsdp"),
        P("fsdp", None),
        P("fsdp", None),
        P("fsdp", None),
        P("fsdp", None),
        P(),
        P(),
        P("fsdp"),
        P("fsdp", None),
        P("fsdp"),
        P("fsdp", None),
        P("fsdp", None),
        P("fsdp", None),
        P("fsdp", "seq", None),
    )
    out_specs = (
        P("fsdp", "seq", None),
        P("fsdp", "seq", None),
        P("fsdp"),
        P("fsdp", "seq"),
        P("fsdp", "seq"),
        P("fsdp", None),
        P("fsdp", None),
        P(),
        P(),
        P("fsdp"),
        P("fsdp", "seq"),
        P("fsdp"),
        P("fsdp", "seq"),
        P("fsdp", "seq"),
        P("fsdp", "seq"),
    )
    return jax.shard_map(
        per_device, mesh=mesh, in_specs=in_specs, out_specs=out_specs, check_vma=False
    )
```
